32 devices in a mesh: occ: 4 (over y, x), vir: 8 (over z, core).
Axes of the slice: x: 2, y: 2, z: 4, core: 2. Of those that a mesh axis runs over, the one named last changes fastest.
Arguments:
- amplitudes: bfloat16 [8, 8, 768, 768], P('occ', None, 'vir'), may hold values from -6 to 6
- integrals: bfloat16 [768, 768], P('vir'), may hold values from -0.21875 to 0.21875
- occ_fock: bfloat16 [8, 8], replicated, may hold values from -2 to 2
- amp_mask: int32 [48, 48], replicated, may hold values 0 or 1
- int_mask: int32 [48, 48], replicated, may hold values 0 or 1
- occ_energy: float32 [8], replicated, may hold values from -2 to -0.5
- vir_energy: float32 [768], replicated, may hold values from 0.5 to 4
Outputs:
- update: float32 [8, 8, 768, 768], P('occ', None, 'vir')
The draws below stay inside these ranges and needn't reach their ends.
All inputs are finite; a program needn't handle non-finite values.
Results may differ from the reference program's by a relative error of at most 0.002.
Values may be sent and summed in bfloat16 or wider, within the bound.
No kernel may reach another device: no remote copies, remote signals or barrier semaphores. Data moves between devices by JAX's collectives and lax.ppermute only.
A program may use at most 128 MiB of HBM per device.

```python
import jax
import jax.numpy as jnp
from jax import lax

V = 768
VB = 16
NO = 8
NVB = 48


def plant(values, stream_key, least, high):
    place = [jax.random.randint(jax.random.fold_in(stream_key, axis), (), 0, length) for axis, length in enumerate(values.shape)]
    main_axis = values.shape.index(max(values.shape))
    next_to = place[:main_axis] + [(place[main_axis] + 1) % values.shape[main_axis]] + place[main_axis + 1:]
    return values.at[tuple(place)].set(least).at[tuple(next_to)].set(high)


def shard_levels(key, dims, cuts, low, top_value):
    factor_of = 1.0
    for dim, blocks in cuts:
        heights = jax.random.uniform(jax.random.fold_in(jax.random.fold_in(key, 6), dim), (blocks,), jnp.float32, low / len(cuts), top_value / len(cuts))
        factor_of = factor_of * jnp.repeat(jnp.exp(heights), dims[dim] // blocks).reshape((-1,) + (1,) * (len(dims) - 1 - dim))
    return factor_of


def centred(key, dims, scale, limit, shards=(), kind=jnp.bfloat16):
    drawn = jax.random.normal(key, dims, jnp.float32) * scale
    if len(shards) > 0:
        drawn = shard_levels(key, dims, shards, -0.22, 0.18) * drawn
    return jnp.clip(drawn, min=-limit, max=limit).astype(kind)


def setup_inputs(seed: int = 0) -> dict:
    key_list = jax.random.split(jax.random.key(seed), 8)
    amplitudes = centred(key_list[0], (NO, NO, V, V), 1.0, 6.0, ((0, 4), (2, 8)))
    integrals = centred(key_list[1], (V, V), V ** -0.5, 0.21875, ((0, 8),))
    occ_fock = centred(key_list[2], (NO, NO), NO ** -0.5, 2.0)
    amp_mask = plant((jax.random.randint(key_list[3], (NVB, NVB), 0, 4) < 3).astype(jnp.int32), jax.random.fold_in(key_list[3], 1), 0, 1)
    int_mask = plant((jax.random.randint(key_list[4], (NVB, NVB), 0, 2) < 1).astype(jnp.int32), jax.random.fold_in(key_list[4], 1), 0, 1)
    occ_energy = jnp.clip(jax.random.uniform(key_list[5], (NO,), jnp.float32, -2.0, -0.5), -2.0, -0.5)
    vir_energy = jnp.clip(jax.random.uniform(key_list[6], (V,), jnp.float32, 0.5, 4.0), 0.5, 4.0)
    return dict(amplitudes=amplitudes, integrals=integrals, occ_fock=occ_fock, amp_mask=amp_mask, int_mask=int_mask, occ_energy=occ_energy, vir_energy=vir_energy)


def expand(mask):
    return jnp.repeat(jnp.repeat(mask, VB, axis=0), VB, axis=1).astype(jnp.bfloat16)


def reference(amplitudes, integrals, occ_fock, amp_mask, int_mask, occ_energy, vir_energy):
    amp_tiles = expand(amp_mask)
    masked_w = integrals * expand(int_mask)
    fock_wide = occ_fock.astype(jnp.float32)

    def one_row(index):
        tile = amplitudes[index] * amp_tiles[None]
        ladder = jnp.dot(tile.reshape(-1, V), masked_w, preferred_element_type=jnp.float32).reshape(NO, V, V)
        holes = jnp.einsum("kab,kj->jab", tile.astype(jnp.float32), fock_wide)
        return ladder + holes

    mixed = lax.map(one_row, jnp.arange(NO))

    def finish(index):
        narrow = mixed[:, index].astype(jnp.bfloat16)
        narrow = lax.optimization_barrier(narrow)
        mirror = narrow.astype(jnp.float32).transpose(0, 2, 1)
        denom = vir_energy[None, :, None] + vir_energy[None, None, :] - occ_energy[index] - occ_energy[:, None, None]
        return (mixed[index] + mirror) / denom

    return lax.map(finish, jnp.arange(NO))
```

```python
import functools

import jax
import jax.numpy as jnp
from jax import lax
from jax.experimental import pallas as pl
from jax.experimental.pallas import tpu as pltpu
from jax.sharding import PartitionSpec as P

CORES = 2
LIMIT = 40 * 1024 * 1024


def expand_rows(mask, first_block, blocks, block):
    rows_here = lax.dynamic_slice_in_dim(mask, first_block, blocks, 0)
    return jnp.repeat(jnp.repeat(rows_here, block, axis=0), block, axis=1).astype(jnp.bfloat16)


def plain(amplitudes, integrals, occ_fock, amp_mask, int_mask, occ_energy, vir_energy):
    occ_rows, occ_all, vir_rows, vir_all = amplitudes.shape
    block = vir_all // amp_mask.shape[0]
    vir_start = lax.axis_index("vir") * vir_rows
    occ_start = lax.axis_index("occ") * occ_rows
    blocks = vir_rows // block
    first_block = vir_start // block
    masked = amplitudes * expand_rows(amp_mask, first_block, blocks, block)[None, None]
    masked_w = integrals * expand_rows(int_mask, first_block, blocks, block)
    flat_amps = masked.reshape(-1, vir_all)
    full_w = lax.all_gather(masked_w, "vir", axis=0, tiled=True)
    ladder = jnp.dot(flat_amps, full_w, preferred_element_type=jnp.float32)
    ladder = ladder.reshape(occ_rows, occ_all, vir_rows, vir_all)
    holes = jnp.einsum("ikab,kj->ijab", masked, occ_fock, preferred_element_type=jnp.float32)
    mixed = ladder + holes
    outgoing = mixed.astype(jnp.bfloat16)
    halfway = lax.all_to_all(outgoing, "vir", split_axis=3, concat_axis=2, tiled=True)
    arrived = lax.all_to_all(halfway, "occ", split_axis=1, concat_axis=0, tiled=True)
    mirrored = arrived.transpose(1, 0, 3, 2).astype(jnp.float32)
    vir_here = lax.dynamic_slice_in_dim(vir_energy, vir_start, vir_rows, 0)
    occ_here = lax.dynamic_slice_in_dim(occ_energy, occ_start, occ_rows, 0)
    denominator = (
        vir_here[None, None, :, None]
        + vir_energy[None, None, None, :]
        - occ_here[:, None, None, None]
        - occ_energy[None, :, None, None]
    )
    return (mixed + mirrored) / denominator


def one_hot(shape, row_of, column_of):
    rows = lax.broadcasted_iota(jnp.int32, shape, 0)
    columns = lax.broadcasted_iota(jnp.int32, shape, 1)
    return (row_of(rows) == column_of(columns)).astype(jnp.float32).astype(jnp.bfloat16)


def mask_kernel(block, meta, amp_mask, int_mask, amp_out, int_out):
    blocks, width = amp_mask.shape[0], int_out.shape[1]
    chip_rows = amp_out.shape[0]
    first = meta[1] * chip_rows
    spread = one_hot((blocks, width), lambda r: r, lambda c: c // block)
    mine = one_hot((chip_rows, blocks), lambda r: (r + first) // block, lambda c: c)
    every = one_hot((width, blocks), lambda r: r // block, lambda c: c)

    def wide(rows, mask):
        tall = jnp.dot(rows, mask[...].astype(jnp.float32).astype(jnp.bfloat16), preferred_element_type=jnp.float32)
        return jnp.dot(tall.astype(jnp.bfloat16), spread, preferred_element_type=jnp.float32).astype(jnp.bfloat16)

    amp_out[...] = wide(mine, amp_mask)
    int_out[...] = wide(every, int_mask)


def gather_kernel(meta, own, near, middle, far, sibling, mask, out):
    rows = own.shape[0]
    z, core = meta[1], meta[2]
    for k, piece in enumerate((own, near, middle, far)):
        for part, at in ((piece[...], core), (sibling[k], 1 - core)):
            start = pl.multiple_of(((z ^ k) * CORES + at) * rows, rows)
            out[pl.ds(start, rows), :] = part * mask[pl.ds(start, rows), :]


def dressing(amps, fock, first_j, i, put):
    occ_rows, occ_all, rows, _ = amps.shape

    def step(s, carry):
        row = pl.multiple_of(s * 16, 16)
        pieces = [amps[i, k, pl.ds(row, 16), :].astype(jnp.float32) for k in range(occ_all)]
        for jj in range(occ_rows):
            total = pieces[0] * fock[0, first_j + jj]
            for k in range(1, occ_all):
                total = total + pieces[k] * fock[k, first_j + jj]
            put(jj, row, total)
        return carry

    lax.fori_loop(0, rows // 16, step, 0)


def send_kernel(meta, fock, own_x, sib_x, own_h, sib_h, w, amp_mask, mask_h, out0, out1, x, h, flipped):
    occ_rows, _, rows, width = own_x.shape
    z, core, first_j = meta[1], meta[2], meta[3] * occ_rows
    for source, holes, at in ((own_x, own_h, core), (sib_x, sib_h, 1 - core)):
        start = pl.multiple_of(at * rows, rows)
        mask = amp_mask[pl.ds(start, rows), :]
        for i in range(occ_rows):
            for jj in range(occ_rows):
                x[i, jj, at] = source[i, jj] * mask

            def put(jj, row, value, i=i, at=at):
                h[i, jj, at, pl.ds(row, 16), :] = value

            dressing(holes, fock, first_j, i, put)
    columns = w.shape[1]
    chip = CORES * rows
    for i in range(occ_rows):
        for jj in range(occ_rows):
            ladder = jnp.dot(x[i, jj].reshape(chip, width), w[...], preferred_element_type=jnp.float32)
            mixed = ladder + h[i, jj].reshape(chip, columns) * mask_h[...].astype(jnp.float32)
            lane = (i * occ_rows + jj) * chip
            flipped[:, lane : lane + chip] = mixed.astype(jnp.bfloat16).T
    for s, out in ((0, out0), (1, out1)):
        start = pl.multiple_of((((z & 1) ^ s) * CORES + core) * rows, rows)
        out[...] = flipped[pl.ds(start, rows), :]


def finish_kernel(meta, fock, occ_energy, own_x, own_h, w_far, w_near, amp_mask, row_energy, all_energy, r0, r1, r2, r3, *rest):
    out, h, arrived = rest[-3:]
    occ_rows, _, rows, width = own_x.shape
    o, z, core, partner = meta[0], meta[1], meta[2], meta[3]
    mask = amp_mask[pl.ds(pl.multiple_of(core * rows, rows), rows), :]
    for k, block in enumerate((r0, r1, r2, r3)):
        arrived[z ^ k] = block[...]
    for i in range(occ_rows):
        def put(jj, row, value, i=i):
            h[i, jj, pl.ds(row, 16), :] = value

        dressing(own_h, fock, partner * occ_rows, i, put)
    x = jnp.concatenate([own_x[i, jj] * mask for i in range(occ_rows) for jj in range(occ_rows)], axis=0)
    half = width // 2
    near_at = z // 2
    chip = CORES * rows
    for side, w in ((0, w_near), (1, w_far)):
        ladder = jnp.dot(x, w[...], preferred_element_type=jnp.float32)
        lanes = pl.ds(pl.multiple_of((near_at ^ side) * half, half), half)
        for i in range(occ_rows):
            for jj in range(occ_rows):
                n = i * occ_rows + jj
                out[i, jj, :, lanes] = ladder[n * rows : (n + 1) * rows]
    for i in range(occ_rows):
        for jj in range(occ_rows):
            lane = (jj * occ_rows + i) * chip
            mirror = jnp.concatenate([arrived[zz, :, lane : lane + chip] for zz in range(width // chip)], axis=1)
            mixed = out[i, jj] + h[i, jj] * mask.astype(jnp.float32)
            below = row_energy[...] + all_energy[...] - occ_energy[o * occ_rows + i] - occ_energy[partner * occ_rows + jj]
            out[i, jj] = (mixed + mirror.astype(jnp.float32)) / below


def whole(shape):
    return pl.BlockSpec(shape, lambda s, meta: (0,) * len(shape))


def paired(occ, vir, amplitudes, integrals, occ_fock, amp_mask, int_mask, occ_energy, vir_energy):
    occ_rows, occ_all, rows, width = amplitudes.shape
    block = width // amp_mask.shape[0]
    chip = CORES * rows
    half = width // 2
    axes = ("occ", "vir")
    o, v = lax.axis_index("occ"), lax.axis_index("vir")
    z, core = v // CORES, v % CORES
    near_at = z // 2
    devices = occ * vir

    def swap(a, k):
        return lax.ppermute(a, axes, [(d, d ^ k) for d in range(devices)])

    def meta(partner=0, side=0):
        return jnp.stack([o, z, core, o ^ partner, near_at ^ side]).astype(jnp.int32)

    params = pltpu.CompilerParams(vmem_limit_bytes=LIMIT)
    smem = pl.BlockSpec(memory_space=pltpu.SMEM)

    def call(kernel, grid_meta, in_specs, out_specs, out_shape, args, scratch=(), aliases={}, flops=0, moved=0):
        return pl.pallas_call(
            kernel,
            grid_spec=pltpu.PrefetchScalarGridSpec(
                num_scalar_prefetch=1, grid=(1,), in_specs=in_specs, out_specs=out_specs, scratch_shapes=list(scratch)
            ),
            out_shape=out_shape,
            input_output_aliases=aliases,
            compiler_params=params,
            cost_estimate=pl.CostEstimate(flops=flops, bytes_accessed=moved, transcendentals=0),
        )(grid_meta, *args)

    bf16, f32 = jnp.bfloat16, jnp.float32
    side_of = [lax.dynamic_slice_in_dim(integrals, (near_at ^ side) * half, half, 1) for side in (0, 1)]
    first = {k: swap(side_of[1 - (k >> 1)], 2 * k) for k in (3, 2, 1)}
    sibling = swap(amplitudes, 1)
    wide_amp, wide_int = call(
        functools.partial(mask_kernel, block),
        meta(),
        [whole(amp_mask.shape), whole(int_mask.shape)],
        [whole((chip, width)), whole((width, width))],
        [jax.ShapeDtypeStruct((chip, width), bf16), jax.ShapeDtypeStruct((width, width), bf16)],
        (amp_mask, int_mask),
    )

    def gathered(own, got, side):
        other = swap(jnp.stack([own, got[1], got[2], got[3]]), 1)
        piece = whole((rows, half))
        return call(
            gather_kernel,
            meta(0, side),
            [piece] * 4 + [whole((4, rows, half)), pl.BlockSpec((width, half), lambda s, m: (0, m[4]))],
            whole((width, half)),
            jax.ShapeDtypeStruct((width, half), bf16),
            (own, got[1], got[2], got[3], other, wide_int),
        )

    fock = occ_fock.astype(f32)

    def tiles(partner, side, w):
        x_spec = pl.BlockSpec((occ_rows, occ_rows, rows, width), lambda s, m: (0, m[3], 0, 0))
        h_spec = pl.BlockSpec((occ_rows, occ_all, rows, half), lambda s, m: (0, 0, 0, m[4]))
        return call(
            send_kernel,
            meta(partner, side),
            [smem, x_spec, x_spec, h_spec, h_spec, whole((width, half)), whole((chip, width)),
             pl.BlockSpec((chip, half), lambda s, m: (0, m[4]))],
            [whole((rows, occ_rows * occ_rows * chip))] * 2,
            [jax.ShapeDtypeStruct((rows, occ_rows * occ_rows * chip), bf16)] * 2,
            (fock, amplitudes, sibling, amplitudes, sibling, w, wide_amp, wide_amp),
            [
                pltpu.VMEM((occ_rows, occ_rows, CORES, rows, width), bf16),
                pltpu.VMEM((occ_rows, occ_rows, CORES, rows, half), f32),
                pltpu.VMEM((half, occ_rows * occ_rows * chip), bf16),
            ],
            flops=2 * occ_rows * occ_rows * chip * width * half,
            moved=8 * 1024 * 1024,
        )

    w_far = gathered(side_of[1], first, 1)
    arrived = {}
    for partner in range(occ):
        t0, t1 = tiles(partner, 1, w_far)
        arrived[partner, 3] = swap(t1, partner * vir + 6)
        arrived[partner, 2] = swap(t0, partner * vir + 4)
    second = {k: swap(side_of[k >> 1], 2 * k) for k in (3, 2, 1)}
    w_near = gathered(side_of[0], second, 0)
    for partner in range(occ):
        t0, t1 = tiles(partner, 0, w_near)
        arrived[partner, 1] = swap(t1, partner * vir + 2)
        arrived[partner, 0] = swap(t0, partner * vir) if partner else t0
    row_energy = lax.dynamic_slice_in_dim(vir_energy, v * rows, rows, 0).reshape(rows, 1)
    all_energy = vir_energy.reshape(1, width)
    out = None
    tile = (rows, occ_rows * occ_rows * chip)
    for partner in range(occ):
        x_spec = pl.BlockSpec((occ_rows, occ_rows, rows, width), lambda s, m: (0, m[3], 0, 0))
        args = [fock, occ_energy, amplitudes, amplitudes, w_far, w_near, wide_amp, row_energy, all_energy]
        specs = [smem, smem, x_spec, whole(amplitudes.shape), whole((width, half)), whole((width, half)),
                 whole((chip, width)), whole((rows, 1)), whole((1, width))]
        args += [arrived[partner, k] for k in range(4)]
        specs += [whole(tile)] * 4
        aliases = {}
        if out is not None:
            aliases = {len(args) + 1: 0}
            args.append(out)
            specs.append(pl.BlockSpec(memory_space=pl.ANY))
        out = call(
            finish_kernel,
            meta(partner),
            specs,
            x_spec,
            jax.ShapeDtypeStruct(amplitudes.shape, f32),
            args,
            [
                pltpu.VMEM((occ_rows, occ_rows, rows, width), f32),
                pltpu.VMEM((4,) + tile, bf16),
            ],
            aliases,
            flops=2 * occ_rows * occ_rows * rows * width * width,
            moved=8 * 1024 * 1024,
        )
    return out


def solution(mesh):
    occ, vir = mesh.shape["occ"], mesh.shape["vir"]

    def local(amplitudes, *others):
        occ_rows, _, rows, width = amplitudes.shape
        fits = (
            occ & (occ - 1) == 0
            and vir == 4 * CORES
            and rows % 16 == 0
            and width % 256 == 0
            and (occ_rows * occ_rows * CORES * rows) % 128 == 0
        )
        if fits:
            return paired(occ, vir, amplitudes, *others)
        return plain(amplitudes, *others)

    in_specs = (P("occ", None, "vir", None), P("vir", None), P(), P(), P(), P(), P())
    out_specs = P("occ", None, "vir", None)
    return jax.shard_map(local, mesh=mesh, in_specs=in_specs, out_specs=out_specs, check_vma=False)
```

```python
import functools

import jax
import jax.numpy as jnp
from jax import lax
from jax.experimental import pallas as pl
from jax.experimental.pallas import tpu as pltpu
from jax.sharding import PartitionSpec as P

CORES = 2
LIMIT = 20 * 1024 * 1024
VMEM = pl.BlockSpec(memory_space=pltpu.VMEM)
SMEM = pl.BlockSpec(memory_space=pltpu.SMEM)


def expand_rows(mask, first_block, blocks, block):
    rows_here = lax.dynamic_slice_in_dim(mask, first_block, blocks, 0)
    return jnp.repeat(jnp.repeat(rows_here, block, axis=0), block, axis=1).astype(jnp.bfloat16)


def plain(amplitudes, integrals, occ_fock, amp_mask, int_mask, occ_energy, vir_energy):
    occ_rows, occ_all, vir_rows, vir_all = amplitudes.shape
    block = vir_all // amp_mask.shape[0]
    vir_start = lax.axis_index("vir") * vir_rows
    occ_start = lax.axis_index("occ") * occ_rows
    blocks = vir_rows // block
    first_block = vir_start // block
    masked = amplitudes * expand_rows(amp_mask, first_block, blocks, block)[None, None]
    masked_w = integrals * expand_rows(int_mask, first_block, blocks, block)
    flat_amps = masked.reshape(-1, vir_all)
    full_w = lax.all_gather(masked_w, "vir", axis=0, tiled=True)
    ladder = jnp.dot(flat_amps, full_w, preferred_element_type=jnp.float32)
    ladder = ladder.reshape(occ_rows, occ_all, vir_rows, vir_all)
    holes = jnp.einsum("ikab,kj->ijab", masked, occ_fock, preferred_element_type=jnp.float32)
    mixed = ladder + holes
    outgoing = mixed.astype(jnp.bfloat16)
    halfway = lax.all_to_all(outgoing, "vir", split_axis=3, concat_axis=2, tiled=True)
    arrived = lax.all_to_all(halfway, "occ", split_axis=1, concat_axis=0, tiled=True)
    mirrored = arrived.transpose(1, 0, 3, 2).astype(jnp.float32)
    vir_here = lax.dynamic_slice_in_dim(vir_energy, vir_start, vir_rows, 0)
    occ_here = lax.dynamic_slice_in_dim(occ_energy, occ_start, occ_rows, 0)
    denominator = (
        vir_here[None, None, :, None]
        + vir_energy[None, None, None, :]
        - occ_here[:, None, None, None]
        - occ_energy[None, :, None, None]
    )
    return (mixed + mirrored) / denominator


def one_hot(shape, row_of, column_of):
    rows = lax.broadcasted_iota(jnp.int32, shape, 0)
    columns = lax.broadcasted_iota(jnp.int32, shape, 1)
    return (row_of(rows) == column_of(columns)).astype(jnp.float32).astype(jnp.bfloat16)


def mask_kernel(block, meta, amp_mask, int_mask, amp_out, int_out):
    blocks, width = amp_mask.shape[0], int_out.shape[1]
    chip_rows = amp_out.shape[0]
    first = meta[1] * chip_rows
    spread = one_hot((blocks, width), lambda r: r, lambda c: c // block)
    mine = one_hot((chip_rows, blocks), lambda r: (r + first) // block, lambda c: c)
    every = one_hot((width, blocks), lambda r: r // block, lambda c: c)

    def wide(rows, mask):
        tall = jnp.dot(rows, mask[...].astype(jnp.float32).astype(jnp.bfloat16), preferred_element_type=jnp.float32)
        return jnp.dot(tall.astype(jnp.bfloat16), spread, preferred_element_type=jnp.float32).astype(jnp.bfloat16)

    amp_out[...] = wide(mine, amp_mask)
    int_out[...] = wide(every, int_mask)


def send_kernel(partner, side, first, carried, *refs):
    meta, fock, own, sib, amp_mask = refs[:5]
    if first:
        pieces, siblings, int_mask, passed = refs[5:9], refs[9:13], refs[13], refs[14 : 14 + carried]
        outs = refs[14 + carried :]
    else:
        w = refs[5]
        outs = refs[7:]
    out0, out1, mixed_out, token = outs[:4]
    x, h, flipped = outs[-3:]
    occ_rows, occ_all, rows, width = own.shape
    half, chip = width // 2, CORES * rows
    o, z, core = meta[0], meta[1], meta[2]
    first_j = (o ^ partner) * occ_rows
    columns = pl.ds(pl.multiple_of(((z // 2) ^ side) * half, half), half)
    if first:
        w = outs[4]
        for k in range(4):
            for piece, at in ((pieces[k], core), (siblings[k], 1 - core)):
                start = pl.multiple_of(((z ^ k) * CORES + at) * rows, rows)
                w[pl.ds(start, rows), :] = piece[...] * int_mask[pl.ds(start, rows), columns]
        for source, copy in zip(passed, outs[5 : 5 + carried], strict=True):
            copy[...] = source[...]
    for source, at in ((own, core), (sib, 1 - core)):
        start = pl.multiple_of(at * rows, rows)
        mask = amp_mask[pl.ds(start, rows), :]
        for i in range(occ_rows):
            for jj in range(occ_rows):
                x[i, jj, at] = source[i, first_j + jj] * mask

        def step(s, carry, source=source, at=at, start=start):
            row = pl.multiple_of(s * 16, 16)
            live = amp_mask[pl.ds(pl.multiple_of(start + row, 16), 16), columns].astype(jnp.float32)
            for i in range(occ_rows):
                amps = [source[i, k, pl.ds(row, 16), columns].astype(jnp.float32) for k in range(occ_all)]
                for jj in range(occ_rows):
                    total = amps[0] * fock[0, first_j + jj]
                    for k in range(1, occ_all):
                        total = total + amps[k] * fock[k, first_j + jj]
                    h[i, jj, at, pl.ds(row, 16), :] = total * live
            return carry

        lax.fori_loop(0, rows // 16, step, 0)
    pairs = occ_rows * occ_rows
    ladder = jnp.dot(x[...].reshape(pairs * chip, width), w[...], preferred_element_type=jnp.float32)
    for i in range(occ_rows):
        for jj in range(occ_rows):
            n = i * occ_rows + jj
            mixed = ladder[n * chip : (n + 1) * chip] + h[i, jj].reshape(chip, half)
            h[i, jj] = mixed.reshape(CORES, rows, half)
            mixed_out[i, jj] = h[i, jj, core]
            flipped[:, n * chip : (n + 1) * chip] = mixed.astype(jnp.bfloat16).T
    for s, out in ((0, out0), (1, out1)):
        start = pl.multiple_of((((z & 1) ^ s) * CORES + core) * rows, rows)
        out[...] = flipped[pl.ds(start, rows), :]
    token[...] = jnp.zeros(token.shape, token.dtype)


def finish_kernel(partner, *refs):
    meta, occ_energy, near, far, row_energy, all_energy, r0, r1, r2, r3 = refs[:10]
    result, tile, sems = refs[-3:]
    occ_rows, _, rows, half = near.shape
    chip = CORES * rows
    o, z = meta[0], meta[1]
    odd = (z & 1) == 1
    first_j = (o ^ partner) * occ_rows
    copies = []
    for i in range(occ_rows):
        for side, mixed, same, other in ((0, near, r0, r1), (1, far, r2, r3)):
            lanes = pl.ds(pl.multiple_of(((z // 2) ^ side) * half, half), half)
            for jj in range(occ_rows):
                lane = (jj * occ_rows + i) * chip
                a, b = same[:, lane : lane + chip], other[:, lane : lane + chip]
                mirror = jnp.concatenate([jnp.where(odd, b, a), jnp.where(odd, a, b)], axis=1)
                below = (
                    row_energy[...] + all_energy[:, lanes] - occ_energy[o * occ_rows + i] - occ_energy[first_j + jj]
                )
                tile[i, jj, :, lanes] = (mixed[i, jj] + mirror.astype(jnp.float32)) / below
        copies.append(pltpu.make_async_copy(tile.at[i], result.at[i, pl.ds(first_j, occ_rows)], sems.at[i]))
        copies[-1].start()
    for copy in copies:
        copy.wait()


def in_vmem(a):
    return pltpu.with_memory_space_constraint(a, pltpu.VMEM)


def paired(occ, vir, amplitudes, integrals, occ_fock, amp_mask, int_mask, occ_energy, vir_energy):
    occ_rows, occ_all, rows, width = amplitudes.shape
    block = width // amp_mask.shape[0]
    chip = CORES * rows
    half = width // 2
    pairs = occ_rows * occ_rows
    axes = ("occ", "vir")
    o, v = lax.axis_index("occ"), lax.axis_index("vir")
    z, core = v // CORES, v % CORES
    near_at = z // 2
    devices = occ * vir
    bf16, f32 = jnp.bfloat16, jnp.float32
    params = pltpu.CompilerParams(vmem_limit_bytes=LIMIT)
    meta = jnp.stack([o, z, core]).astype(jnp.int32)
    fock = occ_fock.astype(f32)

    def swap(a, k):
        return lax.ppermute(a, axes, [(d, d ^ k) for d in range(devices)])

    side_of = [lax.dynamic_slice_in_dim(integrals, (near_at ^ side) * half, half, 1) for side in (0, 1)]
    first = [side_of[1]] + [swap(side_of[1 - (k >> 1)], 2 * k) for k in (1, 2, 3)]
    sibling = swap(amplitudes, 1)
    wide_amp, wide_int = pl.pallas_call(
        functools.partial(mask_kernel, block),
        in_specs=[SMEM, VMEM, VMEM],
        out_specs=[VMEM, VMEM],
        out_shape=[pltpu.VMEM((chip, width), bf16), pltpu.VMEM((width, width), bf16)],
        compiler_params=params,
    )(meta, amp_mask, int_mask)

    def tiles(partner, side, w, token, pieces=None, passed=()):
        args = [meta, fock, in_vmem(amplitudes), in_vmem(sibling), in_vmem(wide_amp)]
        shapes = [
            pltpu.VMEM((rows, pairs * chip), bf16),
            pltpu.VMEM((rows, pairs * chip), bf16),
            pltpu.VMEM((occ_rows, occ_rows, rows, half), f32),
            pltpu.VMEM((8, 128), f32),
        ]
        if pieces is not None:
            args += [in_vmem(a) for a in pieces]
            args += [in_vmem(swap(a, 1)) for a in pieces]
            args += [in_vmem(wide_int)] + [in_vmem(a) for a in passed]
            shapes += [pltpu.VMEM((width, half), bf16)] + [pltpu.VMEM(a.shape, a.dtype) for a in passed]
        else:
            args += [in_vmem(w), in_vmem(token)]
        return pl.pallas_call(
            functools.partial(send_kernel, partner, side, pieces is not None, len(passed)),
            in_specs=[SMEM, SMEM] + [VMEM] * (len(args) - 2),
            out_specs=[VMEM] * len(shapes),
            out_shape=shapes,
            scratch_shapes=[
                pltpu.VMEM((occ_rows, occ_rows, CORES, rows, width), bf16),
                pltpu.VMEM((occ_rows, occ_rows, CORES, rows, half), f32),
                pltpu.VMEM((half, pairs * chip), bf16),
            ],
            compiler_params=params,
            cost_estimate=pl.CostEstimate(
                flops=2 * pairs * chip * width * half, bytes_accessed=8 * 1024 * 1024, transcendentals=0
            ),
        )(*args)

    arrived, mixed, w = {}, {}, {}
    token, again = None, None
    order = [(0, 1), (1, 1), (0, 0), (2, 1), (1, 0), (2, 0), (3, 1), (3, 0)] if occ == 4 else [
        (partner, side) for side in (1, 0) for partner in range(occ)
    ]
    for partner, side in order:
        if (partner, side) == (0, 1):
            t0, t1, mixed[partner, side], token, w[side], *again = tiles(partner, side, None, None, first, side_of)
        elif partner == 0:
            pieces = [again[0]] + [swap(again[k >> 1], 2 * k) for k in (1, 2, 3)]
            t0, t1, mixed[partner, side], token, w[side] = tiles(partner, side, None, None, pieces)
        else:
            t0, t1, mixed[partner, side], token = tiles(partner, side, w[side], token)
        k = 2 * side
        arrived[partner, k + 1] = swap(t1, partner * vir + 2 * (k + 1))
        arrived[partner, k] = swap(t0, partner * vir + 2 * k) if partner or k else t0
    row_energy = lax.dynamic_slice_in_dim(vir_energy, v * rows, rows, 0).reshape(rows, 1)
    all_energy = vir_energy.reshape(1, width)
    out = None
    for partner in range(occ):
        args = [meta, occ_energy, in_vmem(mixed[partner, 0]), in_vmem(mixed[partner, 1]), row_energy, all_energy]
        args += [in_vmem(arrived[partner, k]) for k in range(4)]
        specs = [SMEM, SMEM] + [VMEM] * 8
        aliases = {}
        if out is not None:
            aliases = {len(args): 0}
            args.append(out)
            specs.append(pl.BlockSpec(memory_space=pl.ANY))
        out = pl.pallas_call(
            functools.partial(finish_kernel, partner),
            in_specs=specs,
            out_specs=pl.BlockSpec(memory_space=pl.ANY),
            out_shape=jax.ShapeDtypeStruct(amplitudes.shape, f32),
            scratch_shapes=[pltpu.VMEM((occ_rows, occ_rows, rows, width), f32), pltpu.SemaphoreType.DMA((occ_rows,))],
            input_output_aliases=aliases,
            compiler_params=params,
            cost_estimate=pl.CostEstimate(flops=0, bytes_accessed=4 * 1024 * 1024, transcendentals=0),
        )(*args)
    return out


def solution(mesh):
    occ, vir = mesh.shape["occ"], mesh.shape["vir"]

    def local(amplitudes, *others):
        occ_rows, _, rows, width = amplitudes.shape
        fits = (
            occ & (occ - 1) == 0
            and vir == 4 * CORES
            and rows % 16 == 0
            and width % 256 == 0
            and (occ_rows * occ_rows * CORES * rows) % 128 == 0
        )
        if fits:
            return paired(occ, vir, amplitudes, *others)
        return plain(amplitudes, *others)

    in_specs = (P("occ", None, "vir", None), P("vir", None), P(), P(), P(), P(), P())
    out_specs = P("occ", None, "vir", None)
    return jax.shard_map(local, mesh=mesh, in_specs=in_specs, out_specs=out_specs, check_vma=False)
```

```python
import functools

import jax
import jax.numpy as jnp
from jax import lax
from jax.experimental import pallas as pl
from jax.experimental.pallas import tpu as pltpu
from jax.sharding import PartitionSpec as P

CORES = 2
LIMIT = 12 * 1024 * 1024
VMEM = pl.BlockSpec(memory_space=pltpu.VMEM)
SMEM = pl.BlockSpec(memory_space=pltpu.SMEM)
ANY = pl.BlockSpec(memory_space=pl.ANY)
HBM = pl.BlockSpec(memory_space=pltpu.HBM)


def expand_rows(mask, first_block, blocks, block):
    rows_here = lax.dynamic_slice_in_dim(mask, first_block, blocks, 0)
    return jnp.repeat(jnp.repeat(rows_here, block, axis=0), block, axis=1).astype(jnp.bfloat16)


def plain(amplitudes, integrals, occ_fock, amp_mask, int_mask, occ_energy, vir_energy):
    occ_rows, occ_all, vir_rows, vir_all = amplitudes.shape
    block = vir_all // amp_mask.shape[0]
    vir_start = lax.axis_index("vir") * vir_rows
    occ_start = lax.axis_index("occ") * occ_rows
    blocks = vir_rows // block
    first_block = vir_start // block
    masked = amplitudes * expand_rows(amp_mask, first_block, blocks, block)[None, None]
    masked_w = integrals * expand_rows(int_mask, first_block, blocks, block)
    flat_amps = masked.reshape(-1, vir_all)
    full_w = lax.all_gather(masked_w, "vir", axis=0, tiled=True)
    ladder = jnp.dot(flat_amps, full_w, preferred_element_type=jnp.float32)
    ladder = ladder.reshape(occ_rows, occ_all, vir_rows, vir_all)
    holes = jnp.einsum("ikab,kj->ijab", masked, occ_fock, preferred_element_type=jnp.float32)
    mixed = ladder + holes
    outgoing = mixed.astype(jnp.bfloat16)
    halfway = lax.all_to_all(outgoing, "vir", split_axis=3, concat_axis=2, tiled=True)
    arrived = lax.all_to_all(halfway, "occ", split_axis=1, concat_axis=0, tiled=True)
    mirrored = arrived.transpose(1, 0, 3, 2).astype(jnp.float32)
    vir_here = lax.dynamic_slice_in_dim(vir_energy, vir_start, vir_rows, 0)
    occ_here = lax.dynamic_slice_in_dim(occ_energy, occ_start, occ_rows, 0)
    denominator = (
        vir_here[None, None, :, None]
        + vir_energy[None, None, None, :]
        - occ_here[:, None, None, None]
        - occ_energy[None, :, None, None]
    )
    return (mixed + mirrored) / denominator


def one_hot(shape, row_of, column_of):
    rows = lax.broadcasted_iota(jnp.int32, shape, 0)
    columns = lax.broadcasted_iota(jnp.int32, shape, 1)
    return (row_of(rows) == column_of(columns)).astype(jnp.float32).astype(jnp.bfloat16)


def prepare_kernel(block, meta, fock, own, sib, amp_flags, int_flags, x, h, wide_int, amp_mask, int_mask, sems):
    occ_rows, occ_all, _, rows, width = x.shape
    blocks = amp_mask.shape[0]
    z, core = meta[1], meta[2]
    sources = ((own, core), (sib, 1 - core))
    loads = [pltpu.make_async_copy(source, x.at[:, :, at], sems.at[n]) for n, (source, at) in enumerate(sources)]
    flags = [pltpu.make_async_copy(amp_flags, amp_mask, sems.at[2]), pltpu.make_async_copy(int_flags, int_mask, sems.at[3])]
    for load in flags + loads:
        load.start()
    for load in flags:
        load.wait()
    spread = one_hot((blocks, width), lambda r: r, lambda c: c // block)

    def wide(mask, first):
        rows_of = one_hot((rows, blocks), lambda r: (r + first) // block, lambda c: c)
        tall = jnp.dot(rows_of, mask[...].astype(jnp.float32).astype(jnp.bfloat16), preferred_element_type=jnp.float32)
        return jnp.dot(tall.astype(jnp.bfloat16), spread, preferred_element_type=jnp.float32).astype(jnp.bfloat16)

    for k in range(4):
        wide_int[k] = wide(int_mask, ((z ^ k) * CORES + core) * rows)
    part = width // 2
    for n, (_, at) in enumerate(sources):
        live = wide(amp_mask, (z * CORES + at) * rows)
        loads[n].wait()
        for i in range(occ_rows):
            for j in range(occ_all):
                x[i, j, at] = x[i, j, at] * live

        def step(s, carry, at=at):
            row = pl.multiple_of((s // 2) * 16, 16)
            columns = pl.ds(pl.multiple_of((s % 2) * part, part), part)
            for i in range(occ_rows):
                amps = [x[i, k, at, pl.ds(row, 16), columns].astype(jnp.float32) for k in range(occ_all)]
                for j in range(occ_all):
                    total = amps[0] * fock[0, j]
                    for k in range(1, occ_all):
                        total = total + amps[k] * fock[k, j]
                    h[i, j, at, pl.ds(row, 16), columns] = total
            return carry

        lax.fori_loop(0, 2 * rows // 16, step, 0)


def relay_kernel(own, near, middle, far, mask, out):
    for k, piece in enumerate((own, near, middle, far)):
        out[k] = piece[...] * mask[k]


def tile_kernel(tasks, first, *refs):
    meta, x, h = refs[:3]
    _, occ_all, _, rows, width = x.shape
    half, chip = width // 2, CORES * rows
    o, z, core = meta[0], meta[1], meta[2]
    flipped, own, sems = refs[-3:]
    if first:
        mine, theirs = refs[3:5]
        outs, w = refs[5:-4], refs[-4]
        for k in range(4):
            for piece, at in ((mine, core), (theirs, 1 - core)):
                w[pl.ds(pl.multiple_of(((z ^ k) * CORES + at) * rows, rows), rows), :] = piece[k]
    else:
        w, outs, token = refs[3], refs[5:-4], refs[-4]
        token[...] = jnp.zeros(token.shape, token.dtype)
    occ_rows = own.shape[1]
    pairs = occ_rows * occ_rows
    outs = iter(outs)
    copies = []
    for n, (partner, side) in enumerate(tasks):
        mixed_out = next(outs)
        first_j = (o ^ partner) * occ_rows
        columns = pl.ds(pl.multiple_of(((z // 2) ^ side) * half, half), half)
        ladder = jnp.dot(
            x[:, pl.ds(first_j, occ_rows)].reshape(pairs * chip, width), w[:, columns], preferred_element_type=jnp.float32
        )
        for i in range(occ_rows):
            for jj in range(occ_rows):
                m = i * occ_rows + jj
                mixed = ladder[m * chip : (m + 1) * chip] + h[i, first_j + jj, :, :, columns].reshape(chip, half)
                own[n, i, jj] = mixed.reshape(CORES, rows, half)
                flipped[:, m * chip : (m + 1) * chip] = mixed.astype(jnp.bfloat16).T
        copies.append(pltpu.make_async_copy(own.at[n, :, :, core], mixed_out, sems.at[n]))
        copies[-1].start()
        for s in (0, 1):
            start = pl.multiple_of((((z & 1) ^ s) * CORES + core) * rows, rows)
            next(outs)[...] = flipped[pl.ds(start, rows), :]
    for copy in copies:
        copy.wait()


def finish_kernel(tasks, held, *refs):
    meta, occ_energy, energy = refs[:3]
    count = len(tasks)
    per = [refs[4 + 3 * n : 7 + 3 * n] for n in range(count)]
    result, token = refs[-4:-2] if held else refs[-7:-5]
    if held:
        done, out_sems = refs[-2:]
    else:
        done, out_sems, mixed, tiles, in_sems = refs[-5:]
        loads = []
        for n in range(count):
            targets = [mixed.at[n], tiles.at[n, 0], tiles.at[n, 1]]
            loads.append([pltpu.make_async_copy(per[n][c], targets[c], in_sems.at[n, c]) for c in range(3)])
            for copy in loads[-1]:
                copy.start()
    _, occ_rows, _, rows, half = done.shape
    width, chip = energy.shape[1], CORES * rows
    o, z, core = meta[0], meta[1], meta[2]
    odd = (z & 1) == 1
    place = (z * CORES + core) * rows
    mine = lax.broadcasted_iota(jnp.int32, (rows, width), 1) == lax.broadcasted_iota(jnp.int32, (rows, width), 0) + place
    row_energy = jnp.sum(jnp.where(mine, energy[...], 0.0), axis=1, keepdims=True)
    stores = []
    for n, (partner, side) in enumerate(tasks):
        first_j = (o ^ partner) * occ_rows
        lanes = pl.ds(pl.multiple_of(((z // 2) ^ side) * half, half), half)
        if held:
            own, one, two = per[n]
        else:
            own, one, two = mixed.at[n], tiles.at[n, 0], tiles.at[n, 1]
            for copy in loads[n]:
                copy.wait()
        for i in range(occ_rows):
            for jj in range(occ_rows):
                lane = (jj * occ_rows + i) * chip
                a, b = one[:, lane : lane + chip], two[:, lane : lane + chip]
                mirror = jnp.concatenate([jnp.where(odd, b, a), jnp.where(odd, a, b)], axis=1)
                below = row_energy + energy[:, lanes] - occ_energy[o * occ_rows + i] - occ_energy[first_j + jj]
                done[n, i, jj] = (own[i, jj] + mirror.astype(jnp.float32)) / below
            target = result.at[i, pl.ds(first_j, occ_rows), :, lanes]
            stores.append(pltpu.make_async_copy(done.at[n, i], target, out_sems.at[n, i]))
            stores[-1].start()
    token[...] = jnp.zeros(token.shape, token.dtype)
    for copy in stores:
        copy.wait()


def in_hbm(a):
    return pltpu.with_memory_space_constraint(a, pltpu.HBM)


def in_vmem(a):
    return pltpu.with_memory_space_constraint(a, pltpu.VMEM)


def paired(occ, vir, amplitudes, integrals, occ_fock, amp_mask, int_mask, occ_energy, vir_energy):
    occ_rows, occ_all, rows, width = amplitudes.shape
    block = width // amp_mask.shape[0]
    chip, half, pairs = CORES * rows, width // 2, occ_rows * occ_rows
    axes = ("occ", "vir")
    o, v = lax.axis_index("occ"), lax.axis_index("vir")
    devices = occ * vir
    bf16, f32 = jnp.bfloat16, jnp.float32
    params = pltpu.CompilerParams(vmem_limit_bytes=LIMIT)
    meta = jnp.stack([o, v // CORES, v % CORES]).astype(jnp.int32)
    token_shape = pltpu.VMEM((8, 128), f32)

    def swap(a, k):
        return lax.ppermute(a, axes, [(d, d ^ k) for d in range(devices)])

    def cost(moved):
        return pl.CostEstimate(flops=0, bytes_accessed=moved, transcendentals=0)

    pieces = [integrals] + [swap(integrals, 2 * k) for k in (1, 2, 3)]
    sibling = swap(amplitudes, 1)
    both = (occ_rows, occ_all, CORES, rows, width)
    x, h, wide_int = pl.pallas_call(
        functools.partial(prepare_kernel, block),
        in_specs=[SMEM, SMEM] + [HBM] * 4,
        out_specs=[VMEM] * 3,
        out_shape=[pltpu.VMEM(both, bf16), pltpu.VMEM(both, f32), pltpu.VMEM((4, rows, width), bf16)],
        scratch_shapes=[pltpu.VMEM(a.shape, a.dtype) for a in (amp_mask, int_mask)] + [pltpu.SemaphoreType.DMA((4,))],
        compiler_params=params,
        cost_estimate=cost(1024),
    )(meta, occ_fock.astype(f32), *[in_hbm(a) for a in (amplitudes, sibling, amp_mask, int_mask)])
    relayed = pl.pallas_call(
        relay_kernel,
        in_specs=[VMEM] * 5,
        out_specs=VMEM,
        out_shape=pltpu.VMEM((4, rows, width), bf16),
        compiler_params=params,
        cost_estimate=cost(1024),
    )(*[in_vmem(a) for a in pieces], in_vmem(wide_int))

    tile = (rows, pairs * chip)

    def tiles(tasks, w, token):
        args, specs = [meta, in_vmem(x), in_vmem(h)], [SMEM, VMEM, VMEM]
        shapes, outs = [], []
        for _ in tasks:
            shapes += [jax.ShapeDtypeStruct((occ_rows, occ_rows, rows, half), f32)]
            shapes += [pltpu.VMEM(tile, bf16)] * 2
            outs += [ANY, VMEM, VMEM]
        if w is None:
            args += [in_vmem(relayed), in_vmem(swap(relayed, 1))]
            shapes += [pltpu.VMEM((width, width), bf16)]
        else:
            args += [in_vmem(w), in_vmem(token)]
            shapes += [token_shape]
        made = pl.pallas_call(
            functools.partial(tile_kernel, tasks, w is None),
            in_specs=specs + [VMEM] * (len(args) - 3),
            out_specs=outs + [VMEM],
            out_shape=shapes,
            scratch_shapes=[
                pltpu.VMEM((half, pairs * chip), bf16),
                pltpu.VMEM((len(tasks), occ_rows, occ_rows, CORES, rows, half), f32),
                pltpu.SemaphoreType.DMA((len(tasks),)),
            ],
            compiler_params=params,
            cost_estimate=cost(1024),
        )(*args)
        for n, (partner, side) in enumerate(tasks):
            mixed[partner, side], sends[partner, 2 * side], sends[partner, 2 * side + 1] = made[3 * n : 3 * n + 3]
        arrived.update({(0, 0): sends[0, 0]} if (0, 0) in tasks else {})
        return made[-1]

    def start(which):
        for partner, k in which:
            arrived[partner, k] = swap(sends[partner, k], partner * vir + CORES * k)

    def finish(tasks, passed, out, token, held=False):
        args = [meta, occ_energy, vir_energy.reshape(1, width), in_vmem(token)]
        specs = [SMEM, SMEM, VMEM, VMEM]
        for partner, side in tasks:
            three = (mixed[partner, side], arrived[partner, 2 * side], arrived[partner, 2 * side + 1])
            args += [in_vmem(a) for a in three] if held else three
            specs += [VMEM if held else ANY] * 3
        shapes, outs = [], []
        aliases = {}
        for n, s in enumerate(passed):
            aliases[len(args)] = n
            args.append(in_vmem(sends[s]))
            specs.append(VMEM)
            shapes.append(pltpu.VMEM(sends[s].shape, bf16))
        if out is not None:
            aliases[len(args)] = len(passed)
            args.append(out)
            specs.append(ANY)
        shapes += [jax.ShapeDtypeStruct(amplitudes.shape, f32), token_shape]
        count = len(tasks)
        scratch = [
            pltpu.VMEM((count, occ_rows, occ_rows, rows, half), f32),
            pltpu.SemaphoreType.DMA((count, occ_rows)),
        ]
        if not held:
            scratch += [
                pltpu.VMEM((count, occ_rows, occ_rows, rows, half), f32),
                pltpu.VMEM((count, 2) + tile, bf16),
                pltpu.SemaphoreType.DMA((count, 3)),
            ]
        made = pl.pallas_call(
            functools.partial(finish_kernel, tasks, held),
            in_specs=specs,
            out_specs=[VMEM] * len(passed) + [ANY, VMEM],
            out_shape=shapes,
            scratch_shapes=scratch,
            input_output_aliases=aliases,
            compiler_params=params,
            cost_estimate=cost(1024),
        )(*args)
        for s, a in zip(passed, made):
            sends[s] = a
        return made[len(passed) :]

    arrived, mixed, sends = {}, {}, {}
    w = tiles(((0, 1),), None, None)
    start([(0, 3), (0, 2)])
    token = tiles(((1, 1), (1, 0), (0, 0), (2, 0), (3, 0), (2, 1), (3, 1)), w, sends[0, 2])
    start([(1, 3), (1, 2), (0, 1), (1, 0), (1, 1), (2, 0), (2, 1), (3, 0), (3, 1)])
    out, token = finish(((0, 1),), [(2, 3), (2, 2)], None, token)
    start([(2, 3), (2, 2)])
    out, token = finish(((1, 1), (0, 0), (1, 0)), [(3, 3), (3, 2)], out, token)
    start([(3, 3), (3, 2)])
    out, token = finish(((2, 1), (2, 0), (3, 0)), [], out, token)
    out, token = finish(((3, 1),), [], out, token, True)
    return out


def solution(mesh):
    occ, vir = mesh.shape["occ"], mesh.shape["vir"]

    def local(amplitudes, *others):
        occ_rows, _, rows, width = amplitudes.shape
        fits = (
            occ == 4
            and vir == 4 * CORES
            and rows % 16 == 0
            and width % 256 == 0
            and (occ_rows * occ_rows * CORES * rows) % 128 == 0
        )
        if fits:
            return paired(occ, vir, amplitudes, *others)
        return plain(amplitudes, *others)

    in_specs = (P("occ", None, "vir", None), P("vir", None), P(), P(), P(), P(), P())
    out_specs = P("occ", None, "vir", None)
    return jax.shard_map(local, mesh=mesh, in_specs=in_specs, out_specs=out_specs, check_vma=False)
```

```python
import functools

import jax
import jax.numpy as jnp
from jax import lax
from jax.experimental import pallas as pl
from jax.experimental.pallas import tpu as pltpu
from jax.sharding import PartitionSpec as P

CORES = 2
LIMIT = 12 * 1024 * 1024
VMEM = pl.BlockSpec(memory_space=pltpu.VMEM)
SMEM = pl.BlockSpec(memory_space=pltpu.SMEM)
ANY = pl.BlockSpec(memory_space=pl.ANY)
HBM = pl.BlockSpec(memory_space=pltpu.HBM)


def expand_rows(mask, first_block, blocks, block):
    rows_here = lax.dynamic_slice_in_dim(mask, first_block, blocks, 0)
    return jnp.repeat(jnp.repeat(rows_here, block, axis=0), block, axis=1).astype(jnp.bfloat16)


def plain(amplitudes, integrals, occ_fock, amp_mask, int_mask, occ_energy, vir_energy):
    occ_rows, occ_all, vir_rows, vir_all = amplitudes.shape
    block = vir_all // amp_mask.shape[0]
    vir_start = lax.axis_index("vir") * vir_rows
    occ_start = lax.axis_index("occ") * occ_rows
    blocks = vir_rows // block
    first_block = vir_start // block
    masked = amplitudes * expand_rows(amp_mask, first_block, blocks, block)[None, None]
    masked_w = integrals * expand_rows(int_mask, first_block, blocks, block)
    flat_amps = masked.reshape(-1, vir_all)
    full_w = lax.all_gather(masked_w, "vir", axis=0, tiled=True)
    ladder = jnp.dot(flat_amps, full_w, preferred_element_type=jnp.float32)
    ladder = ladder.reshape(occ_rows, occ_all, vir_rows, vir_all)
    holes = jnp.einsum("ikab,kj->ijab", masked, occ_fock, preferred_element_type=jnp.float32)
    mixed = ladder + holes
    outgoing = mixed.astype(jnp.bfloat16)
    halfway = lax.all_to_all(outgoing, "vir", split_axis=3, concat_axis=2, tiled=True)
    arrived = lax.all_to_all(halfway, "occ", split_axis=1, concat_axis=0, tiled=True)
    mirrored = arrived.transpose(1, 0, 3, 2).astype(jnp.float32)
    vir_here = lax.dynamic_slice_in_dim(vir_energy, vir_start, vir_rows, 0)
    occ_here = lax.dynamic_slice_in_dim(occ_energy, occ_start, occ_rows, 0)
    denominator = (
        vir_here[None, None, :, None]
        + vir_energy[None, None, None, :]
        - occ_here[:, None, None, None]
        - occ_energy[None, :, None, None]
    )
    return (mixed + mirrored) / denominator


def one_hot(shape, row_of, column_of):
    rows = lax.broadcasted_iota(jnp.int32, shape, 0)
    columns = lax.broadcasted_iota(jnp.int32, shape, 1)
    return (row_of(rows) == column_of(columns)).astype(jnp.float32).astype(jnp.bfloat16)


def prepare_kernel(block, meta, fock, own, sib, amp_flags, int_flags, x, h, wide_int, amp_mask, int_mask, sems):
    occ_rows, occ_all, _, rows, width = x.shape
    blocks = amp_mask.shape[0]
    z, core = meta[1], meta[2]
    sources = ((own, core), (sib, 1 - core))
    loads = [pltpu.make_async_copy(source, x.at[:, :, at], sems.at[n]) for n, (source, at) in enumerate(sources)]
    flags = [pltpu.make_async_copy(amp_flags, amp_mask, sems.at[2]), pltpu.make_async_copy(int_flags, int_mask, sems.at[3])]
    for load in flags + loads:
        load.start()
    for load in flags:
        load.wait()
    spread = one_hot((blocks, width), lambda r: r, lambda c: c // block)

    def wide(mask, first):
        rows_of = one_hot((rows, blocks), lambda r: (r + first) // block, lambda c: c)
        tall = jnp.dot(rows_of, mask[...].astype(jnp.float32).astype(jnp.bfloat16), preferred_element_type=jnp.float32)
        return jnp.dot(tall.astype(jnp.bfloat16), spread, preferred_element_type=jnp.float32).astype(jnp.bfloat16)

    for k in range(4):
        wide_int[k] = wide(int_mask, ((z ^ k) * CORES + core) * rows)
    part = width // 2
    for n, (_, at) in enumerate(sources):
        live = wide(amp_mask, (z * CORES + at) * rows)
        loads[n].wait()
        for i in range(occ_rows):
            for j in range(occ_all):
                x[i, j, at] = x[i, j, at] * live

        def step(s, carry, at=at):
            row = pl.multiple_of((s // 2) * 16, 16)
            columns = pl.ds(pl.multiple_of((s % 2) * part, part), part)
            for i in range(occ_rows):
                amps = [x[i, k, at, pl.ds(row, 16), columns].astype(jnp.float32) for k in range(occ_all)]
                for j in range(occ_all):
                    total = amps[0] * fock[0, j]
                    for k in range(1, occ_all):
                        total = total + amps[k] * fock[k, j]
                    h[i, j, at, pl.ds(row, 16), columns] = total
            return carry

        lax.fori_loop(0, 2 * rows // 16, step, 0)


def relay_kernel(own, near, middle, far, mask, out):
    for k, piece in enumerate((own, near, middle, far)):
        out[k] = piece[...] * mask[k]


def make_tiles(makes, r):
    meta, x, h, w, flipped, own, sems = (r[name] for name in ("meta", "x", "h", "w", "flipped", "own", "own_sems"))
    _, occ_rows, _, _, rows, half = own.shape
    width, chip, pairs = x.shape[-1], CORES * rows, occ_rows * occ_rows
    o, z, core = meta[0], meta[1], meta[2]
    copies = []
    for n, (partner, side) in enumerate(makes):
        first_j = (o ^ partner) * occ_rows
        columns = pl.ds(pl.multiple_of(((z // 2) ^ side) * half, half), half)
        ladder = jnp.dot(
            x[:, pl.ds(first_j, occ_rows)].reshape(pairs * chip, width), w[:, columns], preferred_element_type=jnp.float32
        )
        for i in range(occ_rows):
            for jj in range(occ_rows):
                m = i * occ_rows + jj
                mixed = ladder[m * chip : (m + 1) * chip] + h[i, first_j + jj, :, :, columns].reshape(chip, half)
                own[n, i, jj] = mixed.reshape(CORES, rows, half)
                flipped[:, m * chip : (m + 1) * chip] = mixed.astype(jnp.bfloat16).T
        copies.append(pltpu.make_async_copy(own.at[n, :, :, core], r["mixed", partner, side], sems.at[n]))
        copies[-1].start()
        for s in (0, 1):
            start = pl.multiple_of((((z & 1) ^ s) * CORES + core) * rows, rows)
            r["tile", partner, 2 * side + s][...] = flipped[pl.ds(start, rows), :]
    return copies


def finish_tiles(ends, r):
    meta, occ_energy, energy, done, sems = (r[name] for name in ("meta", "occ_energy", "energy", "done", "done_sems"))
    _, occ_rows, _, rows, half = done.shape
    width, chip = energy.shape[1], CORES * rows
    o, z, core = meta[0], meta[1], meta[2]
    odd = (z & 1) == 1
    place = (z * CORES + core) * rows
    mine = lax.broadcasted_iota(jnp.int32, (rows, width), 1) == lax.broadcasted_iota(jnp.int32, (rows, width), 0) + place
    row_energy = jnp.sum(jnp.where(mine, energy[...], 0.0), axis=1, keepdims=True)
    stores = []
    for n, (partner, side) in enumerate(ends):
        first_j = (o ^ partner) * occ_rows
        lanes = pl.ds(pl.multiple_of(((z // 2) ^ side) * half, half), half)
        own, one, two = (r["got", partner, side, c] for c in range(3))
        for i in range(occ_rows):
            for jj in range(occ_rows):
                lane = (jj * occ_rows + i) * chip
                a, b = one[:, lane : lane + chip], two[:, lane : lane + chip]
                mirror = jnp.concatenate([jnp.where(odd, b, a), jnp.where(odd, a, b)], axis=1)
                below = row_energy + energy[:, lanes] - occ_energy[o * occ_rows + i] - occ_energy[first_j + jj]
                done[n, i, jj] = (own[i, jj] + mirror.astype(jnp.float32)) / below
            target = r["result"].at[i, pl.ds(first_j, occ_rows), :, lanes]
            stores.append(pltpu.make_async_copy(done.at[n, i], target, sems.at[n, i]))
            stores[-1].start()
    return stores


def step_kernel(names, makes, ends, *refs):
    r = dict(zip(names, refs, strict=True))
    if "mine" in r:
        z, core = r["meta"][1], r["meta"][2]
        rows = r["mine"].shape[1]
        for k in range(4):
            for piece, at in ((r["mine"], core), (r["theirs"], 1 - core)):
                r["w"][pl.ds(pl.multiple_of(((z ^ k) * CORES + at) * rows, rows), rows), :] = piece[k]
    copies = make_tiles(makes, r) if makes else []
    copies += finish_tiles(ends, r) if ends else []
    r["token"][...] = jnp.zeros(r["token"].shape, r["token"].dtype)
    for copy in copies:
        copy.wait()


def in_hbm(a):
    return pltpu.with_memory_space_constraint(a, pltpu.HBM)


def in_vmem(a):
    return pltpu.with_memory_space_constraint(a, pltpu.VMEM)


def paired(occ, vir, amplitudes, integrals, occ_fock, amp_mask, int_mask, occ_energy, vir_energy):
    occ_rows, occ_all, rows, width = amplitudes.shape
    block = width // amp_mask.shape[0]
    chip, half, pairs = CORES * rows, width // 2, occ_rows * occ_rows
    axes = ("occ", "vir")
    o, v = lax.axis_index("occ"), lax.axis_index("vir")
    devices = occ * vir
    bf16, f32 = jnp.bfloat16, jnp.float32
    params = pltpu.CompilerParams(vmem_limit_bytes=LIMIT)
    meta = jnp.stack([o, v // CORES, v % CORES]).astype(jnp.int32)
    energy = vir_energy.reshape(1, width)
    tile = (rows, pairs * chip)

    def swap(a, k):
        return lax.ppermute(a, axes, [(d, d ^ k) for d in range(devices)])

    pieces = [integrals] + [swap(integrals, CORES * k) for k in (1, 2, 3)]
    sibling = swap(amplitudes, 1)
    both = (occ_rows, occ_all, CORES, rows, width)
    x, h, wide_int = pl.pallas_call(
        functools.partial(prepare_kernel, block),
        in_specs=[SMEM, SMEM] + [HBM] * 4,
        out_specs=[VMEM] * 3,
        out_shape=[pltpu.VMEM(both, bf16), pltpu.VMEM(both, f32), pltpu.VMEM((4, rows, width), bf16)],
        scratch_shapes=[pltpu.VMEM(a.shape, a.dtype) for a in (amp_mask, int_mask)] + [pltpu.SemaphoreType.DMA((4,))],
        compiler_params=params,
    )(meta, occ_fock.astype(f32), *[in_hbm(a) for a in (amplitudes, sibling, amp_mask, int_mask)])
    relayed = pl.pallas_call(
        relay_kernel,
        in_specs=[VMEM] * 5,
        out_specs=VMEM,
        out_shape=pltpu.VMEM((4, rows, width), bf16),
        compiler_params=params,
    )(*[in_vmem(a) for a in pieces], in_vmem(wide_int))

    sends, arrived, mixed, kept = {}, {}, {}, {}

    def step(makes=(), ends=(), passed=()):
        ins, outs, scratch, aliases = [("meta", meta, SMEM)], [], [], {}
        if makes:
            ins += [("x", in_vmem(x), VMEM), ("h", in_vmem(h), VMEM)]
            if "w" in kept:
                ins.append(("w", in_vmem(kept["w"]), VMEM))
            else:
                ins += [("mine", in_vmem(relayed), VMEM), ("theirs", in_vmem(swap(relayed, 1)), VMEM)]
                outs.append(("w", pltpu.VMEM((width, width), bf16), VMEM))
            for partner, side in makes:
                outs.append((("mixed", partner, side), jax.ShapeDtypeStruct((occ_rows, occ_rows, rows, half), f32), ANY))
                outs += [(("tile", partner, 2 * side + s), pltpu.VMEM(tile, bf16), VMEM) for s in (0, 1)]
            scratch += [
                ("flipped", pltpu.VMEM((half, pairs * chip), bf16)),
                ("own", pltpu.VMEM((len(makes), occ_rows, occ_rows, CORES, rows, half), f32)),
                ("own_sems", pltpu.SemaphoreType.DMA((len(makes),))),
            ]
        if ends:
            count = len(ends)
            ins += [("occ_energy", occ_energy, SMEM), ("energy", energy, VMEM)]
            for partner, side in ends:
                got = (mixed[partner, side], arrived[partner, 2 * side], arrived[partner, 2 * side + 1])
                for c, a in enumerate(got):
                    ins.append((("got", partner, side, c), in_vmem(a), VMEM))
            if "result" in kept:
                aliases["partial"] = "result"
                ins.append(("partial", kept["result"], ANY))
            outs.append(("result", jax.ShapeDtypeStruct(amplitudes.shape, f32), ANY))
            scratch += [
                ("done", pltpu.VMEM((count, occ_rows, occ_rows, rows, half), f32)),
                ("done_sems", pltpu.SemaphoreType.DMA((count, occ_rows))),
            ]
        for s in passed:
            aliases["pass", s] = ("passed", s)
            ins.append((("pass", s), in_vmem(sends[s]), VMEM))
            outs.append((("passed", s), pltpu.VMEM(sends[s].shape, bf16), VMEM))
        if "token" in kept:
            ins.append(("before", in_vmem(kept["token"]), VMEM))
        outs.append(("token", pltpu.VMEM((8, 128), f32), VMEM))
        in_names, out_names = [name for name, _, _ in ins], [name for name, _, _ in outs]
        made = pl.pallas_call(
            functools.partial(
                step_kernel, in_names + out_names + [name for name, _ in scratch], tuple(makes), tuple(ends)
            ),
            in_specs=[spec for _, _, spec in ins],
            out_specs=[spec for _, _, spec in outs],
            out_shape=[shape for _, shape, _ in outs],
            scratch_shapes=[shape for _, shape in scratch],
            input_output_aliases={in_names.index(a): out_names.index(b) for a, b in aliases.items()},
            compiler_params=params,
        )(*[a for _, a, _ in ins])
        for name, a in zip(out_names, made, strict=True):
            if name[0] == "mixed":
                mixed[name[1:]] = a
            elif name[0] == "tile":
                sends[name[1:]] = a
            elif name[0] == "passed":
                sends[name[1]] = a
            else:
                kept[name] = a

    def start(which):
        for partner, k in which:
            arrived[partner, k] = swap(sends[partner, k], partner * vir + CORES * k) if partner or k else sends[0, 0]

    step(makes=[(0, 1)])
    start([(0, 3), (0, 2)])
    step(makes=[(1, 1), (0, 0), (1, 0), (2, 0)])
    start([(1, 3), (1, 2), (0, 0), (0, 1), (1, 0), (1, 1), (2, 0)])
    step(makes=[(2, 1), (3, 1), (3, 0)], ends=[(1, 0), (0, 1)], passed=[(2, 1)])
    start([(2, 3), (2, 2), (2, 1), (3, 0)])
    step(ends=[(0, 0), (1, 1)], passed=[(3, 2), (3, 1)])
    start([(3, 2), (3, 1)])
    step(ends=[(2, 1), (2, 0)], passed=[(3, 3)])
    start([(3, 3)])
    step(ends=[(3, 1), (3, 0)])
    return kept["result"]


def solution(mesh):
    occ, vir = mesh.shape["occ"], mesh.shape["vir"]

    def local(amplitudes, *others):
        occ_rows, _, rows, width = amplitudes.shape
        fits = (
            occ == 4
            and vir == 4 * CORES
            and rows % 16 == 0
            and width % 256 == 0
            and (occ_rows * occ_rows * CORES * rows) % 128 == 0
        )
        if fits:
            return paired(occ, vir, amplitudes, *others)
        return plain(amplitudes, *others)

    in_specs = (P("occ", None, "vir", None), P("vir", None), P(), P(), P(), P(), P())
    out_specs = P("occ", None, "vir", None)
    return jax.shard_map(local, mesh=mesh, in_specs=in_specs, out_specs=out_specs, check_vma=False)
```

```python
import functools

import jax
import jax.numpy as jnp
from jax import lax
from jax.experimental import pallas as pl
from jax.experimental.pallas import tpu as pltpu
from jax.sharding import PartitionSpec as P

CORES = 2
LIMIT = 12 * 1024 * 1024
VMEM = pl.BlockSpec(memory_space=pltpu.VMEM)
SMEM = pl.BlockSpec(memory_space=pltpu.SMEM)
ANY = pl.BlockSpec(memory_space=pl.ANY)
HBM = pl.BlockSpec(memory_space=pltpu.HBM)


def expand_rows(mask, first_block, blocks, block):
    rows_here = lax.dynamic_slice_in_dim(mask, first_block, blocks, 0)
    return jnp.repeat(jnp.repeat(rows_here, block, axis=0), block, axis=1).astype(jnp.bfloat16)


def plain(amplitudes, integrals, occ_fock, amp_mask, int_mask, occ_energy, vir_energy):
    occ_rows, occ_all, vir_rows, vir_all = amplitudes.shape
    block = vir_all // amp_mask.shape[0]
    vir_start = lax.axis_index("vir") * vir_rows
    occ_start = lax.axis_index("occ") * occ_rows
    blocks = vir_rows // block
    first_block = vir_start // block
    masked = amplitudes * expand_rows(amp_mask, first_block, blocks, block)[None, None]
    masked_w = integrals * expand_rows(int_mask, first_block, blocks, block)
    flat_amps = masked.reshape(-1, vir_all)
    full_w = lax.all_gather(masked_w, "vir", axis=0, tiled=True)
    ladder = jnp.dot(flat_amps, full_w, preferred_element_type=jnp.float32)
    ladder = ladder.reshape(occ_rows, occ_all, vir_rows, vir_all)
    holes = jnp.einsum("ikab,kj->ijab", masked, occ_fock, preferred_element_type=jnp.float32)
    mixed = ladder + holes
    outgoing = mixed.astype(jnp.bfloat16)
    halfway = lax.all_to_all(outgoing, "vir", split_axis=3, concat_axis=2, tiled=True)
    arrived = lax.all_to_all(halfway, "occ", split_axis=1, concat_axis=0, tiled=True)
    mirrored = arrived.transpose(1, 0, 3, 2).astype(jnp.float32)
    vir_here = lax.dynamic_slice_in_dim(vir_energy, vir_start, vir_rows, 0)
    occ_here = lax.dynamic_slice_in_dim(occ_energy, occ_start, occ_rows, 0)
    denominator = (
        vir_here[None, None, :, None]
        + vir_energy[None, None, None, :]
        - occ_here[:, None, None, None]
        - occ_energy[None, :, None, None]
    )
    return (mixed + mirrored) / denominator


def one_hot(shape, row_of, column_of):
    rows = lax.broadcasted_iota(jnp.int32, shape, 0)
    columns = lax.broadcasted_iota(jnp.int32, shape, 1)
    return (row_of(rows) == column_of(columns)).astype(jnp.float32).astype(jnp.bfloat16)


def prepare_kernel(block, meta, fock, own, sib, amp_flags, int_flags, x, h, wide_int, amp_mask, int_mask, sems):
    occ_rows, occ_all, _, rows, width = x.shape
    blocks = amp_mask.shape[0]
    z, core = meta[1], meta[2]
    sources = ((own, core), (sib, 1 - core))
    loads = [pltpu.make_async_copy(source, x.at[:, :, at], sems.at[n]) for n, (source, at) in enumerate(sources)]
    flags = [pltpu.make_async_copy(amp_flags, amp_mask, sems.at[2]), pltpu.make_async_copy(int_flags, int_mask, sems.at[3])]
    for load in flags + loads:
        load.start()
    for load in flags:
        load.wait()
    spread = one_hot((blocks, width), lambda r: r, lambda c: c // block)

    def wide(mask, first):
        rows_of = one_hot((rows, blocks), lambda r: (r + first) // block, lambda c: c)
        tall = jnp.dot(rows_of, mask[...].astype(jnp.float32).astype(jnp.bfloat16), preferred_element_type=jnp.float32)
        return jnp.dot(tall.astype(jnp.bfloat16), spread, preferred_element_type=jnp.float32).astype(jnp.bfloat16)

    for k in range(4):
        wide_int[k] = wide(int_mask, ((z ^ k) * CORES + core) * rows)
    part = width // 2
    for n, (_, at) in enumerate(sources):
        live = wide(amp_mask, (z * CORES + at) * rows)
        loads[n].wait()
        for i in range(occ_rows):
            for j in range(occ_all):
                x[i, j, at] = x[i, j, at] * live

        def step(s, carry, at=at):
            row = pl.multiple_of((s // 2) * 16, 16)
            columns = pl.ds(pl.multiple_of((s % 2) * part, part), part)
            for i in range(occ_rows):
                amps = [x[i, k, at, pl.ds(row, 16), columns].astype(jnp.float32) for k in range(occ_all)]
                for j in range(occ_all):
                    total = amps[0] * fock[0, j]
                    for k in range(1, occ_all):
                        total = total + amps[k] * fock[k, j]
                    h[i, j, at, pl.ds(row, 16), columns] = total
            return carry

        lax.fori_loop(0, 2 * rows // 16, step, 0)


def half_of(z, side, half):
    return pl.ds(pl.multiple_of(((z // 2) ^ side) * half, half), half)


def relay_kernel(meta, own, near, middle, far, mask, near_out, far_out):
    half = near_out.shape[-1]
    for side, out in ((0, near_out), (1, far_out)):
        columns = half_of(meta[1], side, half)
        for k, piece in enumerate((own, near, middle, far)):
            out[k] = piece[:, columns] * mask[k, :, columns]


def make_tiles(makes, r):
    meta, x, h, flipped, own, sems = (r[name] for name in ("meta", "x", "h", "flipped", "own", "own_sems"))
    _, occ_rows, _, _, rows, half = own.shape
    width, chip, pairs = x.shape[-1], CORES * rows, occ_rows * occ_rows
    o, z, core = meta[0], meta[1], meta[2]
    copies = []
    for n, (partner, side) in enumerate(makes):
        first_j = (o ^ partner) * occ_rows
        columns = half_of(z, side, half)
        ladder = jnp.dot(
            x[:, pl.ds(first_j, occ_rows)].reshape(pairs * chip, width),
            r["w", side][...],
            preferred_element_type=jnp.float32,
        )
        for i in range(occ_rows):
            for jj in range(occ_rows):
                m = i * occ_rows + jj
                mixed = ladder[m * chip : (m + 1) * chip] + h[i, first_j + jj, :, :, columns].reshape(chip, half)
                own[n, i, jj] = mixed.reshape(CORES, rows, half)
                flipped[:, m * chip : (m + 1) * chip] = mixed.astype(jnp.bfloat16).T
        copies.append(pltpu.make_async_copy(own.at[n, :, :, core], r["mixed", partner, side], sems.at[n]))
        copies[-1].start()
        for s in (0, 1):
            start = pl.multiple_of((((z & 1) ^ s) * CORES + core) * rows, rows)
            r["tile", partner, 2 * side + s][...] = flipped[pl.ds(start, rows), :]
    return copies


def finish_tiles(ends, r):
    meta, occ_energy, energy, done, sems = (r[name] for name in ("meta", "occ_energy", "energy", "done", "done_sems"))
    _, occ_rows, _, rows, half = done.shape
    width, chip = energy.shape[1], CORES * rows
    o, z, core = meta[0], meta[1], meta[2]
    odd = (z & 1) == 1
    place = (z * CORES + core) * rows
    mine = lax.broadcasted_iota(jnp.int32, (rows, width), 1) == lax.broadcasted_iota(jnp.int32, (rows, width), 0) + place
    row_energy = jnp.sum(jnp.where(mine, energy[...], 0.0), axis=1, keepdims=True)
    stores = []
    for n, (partner, side) in enumerate(ends):
        first_j = (o ^ partner) * occ_rows
        lanes = half_of(z, side, half)
        own, one, two = (r["got", partner, side, c] for c in range(3))
        for i in range(occ_rows):
            for jj in range(occ_rows):
                lane = (jj * occ_rows + i) * chip
                a, b = one[:, lane : lane + chip], two[:, lane : lane + chip]
                mirror = jnp.concatenate([jnp.where(odd, b, a), jnp.where(odd, a, b)], axis=1)
                below = row_energy + energy[:, lanes] - occ_energy[o * occ_rows + i] - occ_energy[first_j + jj]
                done[n, i, jj] = (own[i, jj] + mirror.astype(jnp.float32)) / below
            target = r["result"].at[i, pl.ds(first_j, occ_rows), :, lanes]
            stores.append(pltpu.make_async_copy(done.at[n, i], target, sems.at[n, i]))
            stores[-1].start()
    return stores


def step_kernel(names, makes, ends, *refs):
    r = dict(zip(names, refs, strict=True))
    for side in (0, 1):
        if ("mine", side) in r:
            z, core = r["meta"][1], r["meta"][2]
            rows = r["mine", side].shape[1]
            for k in range(4):
                for piece, at in ((r["mine", side], core), (r["theirs", side], 1 - core)):
                    start = pl.multiple_of(((z ^ k) * CORES + at) * rows, rows)
                    r["w", side][pl.ds(start, rows), :] = piece[k]
    copies = make_tiles(makes, r) if makes else []
    copies += finish_tiles(ends, r) if ends else []
    r["token"][...] = jnp.zeros(r["token"].shape, r["token"].dtype)
    for copy in copies:
        copy.wait()


def in_hbm(a):
    return pltpu.with_memory_space_constraint(a, pltpu.HBM)


def in_vmem(a):
    return pltpu.with_memory_space_constraint(a, pltpu.VMEM)


def paired(occ, vir, amplitudes, integrals, occ_fock, amp_mask, int_mask, occ_energy, vir_energy):
    occ_rows, occ_all, rows, width = amplitudes.shape
    block = width // amp_mask.shape[0]
    chip, half, pairs = CORES * rows, width // 2, occ_rows * occ_rows
    axes = ("occ", "vir")
    o, v = lax.axis_index("occ"), lax.axis_index("vir")
    devices = occ * vir
    bf16, f32 = jnp.bfloat16, jnp.float32
    params = pltpu.CompilerParams(vmem_limit_bytes=LIMIT)
    meta = jnp.stack([o, v // CORES, v % CORES]).astype(jnp.int32)
    energy = vir_energy.reshape(1, width)
    tile = (rows, pairs * chip)

    def swap(a, k):
        return lax.ppermute(a, axes, [(d, d ^ k) for d in range(devices)])

    pieces = [integrals] + [swap(integrals, CORES * k) for k in (1, 2, 3)]
    sibling = swap(amplitudes, 1)
    both = (occ_rows, occ_all, CORES, rows, width)
    x, h, wide_int = pl.pallas_call(
        functools.partial(prepare_kernel, block),
        in_specs=[SMEM, SMEM] + [HBM] * 4,
        out_specs=[VMEM] * 3,
        out_shape=[pltpu.VMEM(both, bf16), pltpu.VMEM(both, f32), pltpu.VMEM((4, rows, width), bf16)],
        scratch_shapes=[pltpu.VMEM(a.shape, a.dtype) for a in (amp_mask, int_mask)] + [pltpu.SemaphoreType.DMA((4,))],
        compiler_params=params,
    )(meta, occ_fock.astype(f32), *[in_hbm(a) for a in (amplitudes, sibling, amp_mask, int_mask)])
    relayed = pl.pallas_call(
        relay_kernel,
        in_specs=[SMEM] + [VMEM] * 5,
        out_specs=[VMEM] * 2,
        out_shape=[pltpu.VMEM((4, rows, half), bf16)] * 2,
        compiler_params=params,
    )(meta, *[in_vmem(a) for a in pieces], in_vmem(wide_int))

    sends, arrived, mixed, kept = {}, {}, {}, {}

    def step(makes=(), ends=(), passed=()):
        ins, outs, scratch, aliases = [("meta", meta, SMEM)], [], [], {}
        if makes:
            ins += [("x", in_vmem(x), VMEM), ("h", in_vmem(h), VMEM)]
            for side in sorted({side for _, side in makes}):
                if ("w", side) in kept:
                    ins.append((("w", side), in_vmem(kept["w", side]), VMEM))
                else:
                    ins.append((("mine", side), in_vmem(relayed[side]), VMEM))
                    ins.append((("theirs", side), in_vmem(swap(relayed[side], 1)), VMEM))
                    outs.append((("w", side), pltpu.VMEM((width, half), bf16), VMEM))
            for partner, side in makes:
                outs.append((("mixed", partner, side), jax.ShapeDtypeStruct((occ_rows, occ_rows, rows, half), f32), ANY))
                outs += [(("tile", partner, 2 * side + s), pltpu.VMEM(tile, bf16), VMEM) for s in (0, 1)]
            scratch += [
                ("flipped", pltpu.VMEM((half, pairs * chip), bf16)),
                ("own", pltpu.VMEM((len(makes), occ_rows, occ_rows, CORES, rows, half), f32)),
                ("own_sems", pltpu.SemaphoreType.DMA((len(makes),))),
            ]
        if ends:
            count = len(ends)
            ins += [("occ_energy", occ_energy, SMEM), ("energy", energy, VMEM)]
            for partner, side in ends:
                got = (mixed[partner, side], arrived[partner, 2 * side], arrived[partner, 2 * side + 1])
                for c, a in enumerate(got):
                    ins.append((("got", partner, side, c), in_vmem(a), VMEM))
            if "result" in kept:
                aliases["partial"] = "result"
                ins.append(("partial", kept["result"], ANY))
            outs.append(("result", jax.ShapeDtypeStruct(amplitudes.shape, f32), ANY))
            scratch += [
                ("done", pltpu.VMEM((count, occ_rows, occ_rows, rows, half), f32)),
                ("done_sems", pltpu.SemaphoreType.DMA((count, occ_rows))),
            ]
        for s in passed:
            aliases["pass", s] = ("passed", s)
            ins.append((("pass", s), in_vmem(sends[s]), VMEM))
            outs.append((("passed", s), pltpu.VMEM(sends[s].shape, bf16), VMEM))
        if "token" in kept:
            ins.append(("before", in_vmem(kept["token"]), VMEM))
        outs.append(("token", pltpu.VMEM((8, 128), f32), VMEM))
        in_names, out_names = [name for name, _, _ in ins], [name for name, _, _ in outs]
        made = pl.pallas_call(
            functools.partial(
                step_kernel, in_names + out_names + [name for name, _ in scratch], tuple(makes), tuple(ends)
            ),
            in_specs=[spec for _, _, spec in ins],
            out_specs=[spec for _, _, spec in outs],
            out_shape=[shape for _, shape, _ in outs],
            scratch_shapes=[shape for _, shape in scratch],
            input_output_aliases={in_names.index(a): out_names.index(b) for a, b in aliases.items()},
            compiler_params=params,
        )(*[a for _, a, _ in ins])
        for name, a in zip(out_names, made, strict=True):
            if name[0] == "mixed":
                mixed[name[1:]] = a
            elif name[0] == "tile":
                sends[name[1:]] = a
            elif name[0] == "passed":
                sends[name[1]] = a
            else:
                kept[name] = a

    def start(which):
        for partner, k in which:
            arrived[partner, k] = swap(sends[partner, k], partner * vir + CORES * k) if partner or k else sends[0, 0]

    step(makes=[(0, 1)])
    start([(0, 3), (0, 2)])
    step(makes=[(1, 1), (0, 0), (1, 0), (2, 0)])
    start([(1, 3), (1, 2), (0, 0), (0, 1), (1, 0), (1, 1), (2, 0)])
    step(makes=[(2, 1), (3, 1), (3, 0)], ends=[(1, 0), (0, 1)], passed=[(2, 1)])
    start([(2, 3), (2, 2), (2, 1), (3, 0)])
    step(ends=[(0, 0), (1, 1)], passed=[(3, 2), (3, 1)])
    start([(3, 2), (3, 1)])
    step(ends=[(2, 1), (2, 0)], passed=[(3, 3)])
    start([(3, 3)])
    step(ends=[(3, 1), (3, 0)])
    return kept["result"]


def solution(mesh):
    occ, vir = mesh.shape["occ"], mesh.shape["vir"]

    def local(amplitudes, *others):
        occ_rows, _, rows, width = amplitudes.shape
        fits = (
            occ == 4
            and vir == 4 * CORES
            and rows % 16 == 0
            and width % 256 == 0
            and (occ_rows * occ_rows * CORES * rows) % 128 == 0
        )
        if fits:
            return paired(occ, vir, amplitudes, *others)
        return plain(amplitudes, *others)

    in_specs = (P("occ", None, "vir", None), P("vir", None), P(), P(), P(), P(), P())
    out_specs = P("occ", None, "vir", None)
    return jax.shard_map(local, mesh=mesh, in_specs=in_specs, out_specs=out_specs, check_vma=False)
```

```python
import functools

import jax
import jax.numpy as jnp
from jax import lax
from jax.experimental import pallas as pl
from jax.experimental.pallas import tpu as pltpu
from jax.sharding import PartitionSpec as P

CORES = 2
LIMIT = 12 * 1024 * 1024
VMEM = pl.BlockSpec(memory_space=pltpu.VMEM)
SMEM = pl.BlockSpec(memory_space=pltpu.SMEM)
ANY = pl.BlockSpec(memory_space=pl.ANY)
HBM = pl.BlockSpec(memory_space=pltpu.HBM)


def expand_rows(mask, first_block, blocks, block):
    rows_here = lax.dynamic_slice_in_dim(mask, first_block, blocks, 0)
    return jnp.repeat(jnp.repeat(rows_here, block, axis=0), block, axis=1).astype(jnp.bfloat16)


def plain(amplitudes, integrals, occ_fock, amp_mask, int_mask, occ_energy, vir_energy):
    occ_rows, occ_all, vir_rows, vir_all = amplitudes.shape
    block = vir_all // amp_mask.shape[0]
    vir_start = lax.axis_index("vir") * vir_rows
    occ_start = lax.axis_index("occ") * occ_rows
    blocks = vir_rows // block
    first_block = vir_start // block
    masked = amplitudes * expand_rows(amp_mask, first_block, blocks, block)[None, None]
    masked_w = integrals * expand_rows(int_mask, first_block, blocks, block)
    flat_amps = masked.reshape(-1, vir_all)
    full_w = lax.all_gather(masked_w, "vir", axis=0, tiled=True)
    ladder = jnp.dot(flat_amps, full_w, preferred_element_type=jnp.float32)
    ladder = ladder.reshape(occ_rows, occ_all, vir_rows, vir_all)
    holes = jnp.einsum("ikab,kj->ijab", masked, occ_fock, preferred_element_type=jnp.float32)
    mixed = ladder + holes
    outgoing = mixed.astype(jnp.bfloat16)
    halfway = lax.all_to_all(outgoing, "vir", split_axis=3, concat_axis=2, tiled=True)
    arrived = lax.all_to_all(halfway, "occ", split_axis=1, concat_axis=0, tiled=True)
    mirrored = arrived.transpose(1, 0, 3, 2).astype(jnp.float32)
    vir_here = lax.dynamic_slice_in_dim(vir_energy, vir_start, vir_rows, 0)
    occ_here = lax.dynamic_slice_in_dim(occ_energy, occ_start, occ_rows, 0)
    denominator = (
        vir_here[None, None, :, None]
        + vir_energy[None, None, None, :]
        - occ_here[:, None, None, None]
        - occ_energy[None, :, None, None]
    )
    return (mixed + mirrored) / denominator


def one_hot(shape, row_of, column_of):
    rows = lax.broadcasted_iota(jnp.int32, shape, 0)
    columns = lax.broadcasted_iota(jnp.int32, shape, 1)
    return (row_of(rows) == column_of(columns)).astype(jnp.float32).astype(jnp.bfloat16)


def prepare_kernel(block, meta, fock, own, sib, amp_flags, int_flags, x, h, wide_int, amp_mask, int_mask, sems):
    occ_rows, occ_all, _, rows, width = x.shape
    blocks = amp_mask.shape[0]
    z, core = meta[1], meta[2]
    sources = ((own, core), (sib, 1 - core))
    loads = [pltpu.make_async_copy(source, x.at[:, :, at], sems.at[n]) for n, (source, at) in enumerate(sources)]
    flags = [pltpu.make_async_copy(amp_flags, amp_mask, sems.at[2]), pltpu.make_async_copy(int_flags, int_mask, sems.at[3])]
    for load in flags + loads:
        load.start()
    for load in flags:
        load.wait()
    spread = one_hot((blocks, width), lambda r: r, lambda c: c // block)

    def wide(mask, first):
        rows_of = one_hot((rows, blocks), lambda r: (r + first) // block, lambda c: c)
        tall = jnp.dot(rows_of, mask[...].astype(jnp.float32).astype(jnp.bfloat16), preferred_element_type=jnp.float32)
        return jnp.dot(tall.astype(jnp.bfloat16), spread, preferred_element_type=jnp.float32).astype(jnp.bfloat16)

    for k in range(4):
        wide_int[k] = wide(int_mask, ((z ^ k) * CORES + core) * rows)
    part = width // 2
    for n, (_, at) in enumerate(sources):
        live = wide(amp_mask, (z * CORES + at) * rows)
        loads[n].wait()
        for i in range(occ_rows):
            for j in range(occ_all):
                x[i, j, at] = x[i, j, at] * live

        def step(s, carry, at=at):
            row = pl.multiple_of((s // 2) * 16, 16)
            columns = pl.ds(pl.multiple_of((s % 2) * part, part), part)
            for i in range(occ_rows):
                amps = [x[i, k, at, pl.ds(row, 16), columns].astype(jnp.float32) for k in range(occ_all)]
                for j in range(occ_all):
                    total = amps[0] * fock[0, j]
                    for k in range(1, occ_all):
                        total = total + amps[k] * fock[k, j]
                    h[i, j, at, pl.ds(row, 16), columns] = total
            return carry

        lax.fori_loop(0, 2 * rows // 16, step, 0)


def relay_kernel(own, near, middle, far, mask, out):
    for k, piece in enumerate((own, near, middle, far)):
        out[k] = piece[...] * mask[k]


def make_tiles(makes, r):
    meta, x, h, w, flipped, own = (r[name] for name in ("meta", "x", "h", "w", "flipped", "own"))
    occ_rows, _, _, rows, half = own.shape
    width, chip, pairs = x.shape[-1], CORES * rows, occ_rows * occ_rows
    o, z, core = meta[0], meta[1], meta[2]
    for partner, side in makes:
        first_j = (o ^ partner) * occ_rows
        columns = pl.ds(pl.multiple_of(((z // 2) ^ side) * half, half), half)
        ladder = jnp.dot(
            x[:, pl.ds(first_j, occ_rows)].reshape(pairs * chip, width), w[:, columns], preferred_element_type=jnp.float32
        )
        for i in range(occ_rows):
            for jj in range(occ_rows):
                m = i * occ_rows + jj
                mixed = ladder[m * chip : (m + 1) * chip] + h[i, first_j + jj, :, :, columns].reshape(chip, half)
                own[i, jj] = mixed.reshape(CORES, rows, half)
                r["mixed", partner, side][i, jj] = own[i, jj, core]
                flipped[:, m * chip : (m + 1) * chip] = mixed.astype(jnp.bfloat16).T
        for s in (0, 1):
            start = pl.multiple_of((((z & 1) ^ s) * CORES + core) * rows, rows)
            r["tile", partner, 2 * side + s][...] = flipped[pl.ds(start, rows), :]


def finish_tiles(ends, r):
    meta, occ_energy, energy, done, sems = (r[name] for name in ("meta", "occ_energy", "energy", "done", "done_sems"))
    _, occ_rows, _, rows, half = done.shape
    width, chip = energy.shape[1], CORES * rows
    o, z, core = meta[0], meta[1], meta[2]
    odd = (z & 1) == 1
    place = (z * CORES + core) * rows
    mine = lax.broadcasted_iota(jnp.int32, (rows, width), 1) == lax.broadcasted_iota(jnp.int32, (rows, width), 0) + place
    row_energy = jnp.sum(jnp.where(mine, energy[...], 0.0), axis=1, keepdims=True)
    stores = []
    for n, (partner, side) in enumerate(ends):
        first_j = (o ^ partner) * occ_rows
        lanes = pl.ds(pl.multiple_of(((z // 2) ^ side) * half, half), half)
        own, one, two = (r["got", partner, side, c] for c in range(3))
        for i in range(occ_rows):
            for jj in range(occ_rows):
                lane = (jj * occ_rows + i) * chip
                a, b = one[:, lane : lane + chip], two[:, lane : lane + chip]
                mirror = jnp.concatenate([jnp.where(odd, b, a), jnp.where(odd, a, b)], axis=1)
                below = row_energy + energy[:, lanes] - occ_energy[o * occ_rows + i] - occ_energy[first_j + jj]
                done[n, i, jj] = (own[i, jj] + mirror.astype(jnp.float32)) / below
            target = r["result"].at[i, pl.ds(first_j, occ_rows), :, lanes]
            stores.append(pltpu.make_async_copy(done.at[n, i], target, sems.at[n, i]))
            stores[-1].start()
    return stores


def step_kernel(names, makes, ends, *refs):
    r = dict(zip(names, refs, strict=True))
    if "mine" in r:
        z, core = r["meta"][1], r["meta"][2]
        rows = r["mine"].shape[1]
        for k in range(4):
            for piece, at in ((r["mine"], core), (r["theirs"], 1 - core)):
                r["w"][pl.ds(pl.multiple_of(((z ^ k) * CORES + at) * rows, rows), rows), :] = piece[k]
    if makes:
        make_tiles(makes, r)
    copies = finish_tiles(ends, r) if ends else []
    r["token"][...] = jnp.zeros(r["token"].shape, r["token"].dtype)
    for copy in copies:
        copy.wait()


def in_hbm(a):
    return pltpu.with_memory_space_constraint(a, pltpu.HBM)


def in_vmem(a):
    return pltpu.with_memory_space_constraint(a, pltpu.VMEM)


def paired(occ, vir, amplitudes, integrals, occ_fock, amp_mask, int_mask, occ_energy, vir_energy):
    occ_rows, occ_all, rows, width = amplitudes.shape
    block = width // amp_mask.shape[0]
    chip, half, pairs = CORES * rows, width // 2, occ_rows * occ_rows
    axes = ("occ", "vir")
    o, v = lax.axis_index("occ"), lax.axis_index("vir")
    devices = occ * vir
    bf16, f32 = jnp.bfloat16, jnp.float32
    params = pltpu.CompilerParams(vmem_limit_bytes=LIMIT)
    meta = jnp.stack([o, v // CORES, v % CORES]).astype(jnp.int32)
    energy = vir_energy.reshape(1, width)
    tile = (rows, pairs * chip)

    def swap(a, k):
        return lax.ppermute(a, axes, [(d, d ^ k) for d in range(devices)])

    pieces = [integrals] + [swap(integrals, CORES * k) for k in (1, 2, 3)]
    sibling = swap(amplitudes, 1)
    both = (occ_rows, occ_all, CORES, rows, width)
    x, h, wide_int = pl.pallas_call(
        functools.partial(prepare_kernel, block),
        in_specs=[SMEM, SMEM] + [HBM] * 4,
        out_specs=[VMEM] * 3,
        out_shape=[pltpu.VMEM(both, bf16), pltpu.VMEM(both, f32), pltpu.VMEM((4, rows, width), bf16)],
        scratch_shapes=[pltpu.VMEM(a.shape, a.dtype) for a in (amp_mask, int_mask)] + [pltpu.SemaphoreType.DMA((4,))],
        compiler_params=params,
    )(meta, occ_fock.astype(f32), *[in_hbm(a) for a in (amplitudes, sibling, amp_mask, int_mask)])
    relayed = pl.pallas_call(
        relay_kernel,
        in_specs=[VMEM] * 5,
        out_specs=VMEM,
        out_shape=pltpu.VMEM((4, rows, width), bf16),
        compiler_params=params,
    )(*[in_vmem(a) for a in pieces], in_vmem(wide_int))

    sends, arrived, mixed, kept = {}, {}, {}, {}

    def step(makes=(), ends=(), passed=()):
        ins, outs, scratch, aliases = [("meta", meta, SMEM)], [], [], {}
        if makes:
            ins += [("x", in_vmem(x), VMEM), ("h", in_vmem(h), VMEM)]
            if "w" in kept:
                ins.append(("w", in_vmem(kept["w"]), VMEM))
            else:
                ins += [("mine", in_vmem(relayed), VMEM), ("theirs", in_vmem(swap(relayed, 1)), VMEM)]
                outs.append(("w", pltpu.VMEM((width, width), bf16), VMEM))
            for partner, side in makes:
                outs.append((("mixed", partner, side), pltpu.VMEM((occ_rows, occ_rows, rows, half), f32), VMEM))
                outs += [(("tile", partner, 2 * side + s), pltpu.VMEM(tile, bf16), VMEM) for s in (0, 1)]
            scratch += [
                ("flipped", pltpu.VMEM((half, pairs * chip), bf16)),
                ("own", pltpu.VMEM((occ_rows, occ_rows, CORES, rows, half), f32)),
            ]
        if ends:
            count = len(ends)
            ins += [("occ_energy", occ_energy, SMEM), ("energy", energy, VMEM)]
            for partner, side in ends:
                got = (mixed[partner, side], arrived[partner, 2 * side], arrived[partner, 2 * side + 1])
                for c, a in enumerate(got):
                    ins.append((("got", partner, side, c), in_vmem(a), VMEM))
            if "result" in kept:
                aliases["partial"] = "result"
                ins.append(("partial", kept["result"], ANY))
            outs.append(("result", jax.ShapeDtypeStruct(amplitudes.shape, f32), ANY))
            scratch += [
                ("done", pltpu.VMEM((count, occ_rows, occ_rows, rows, half), f32)),
                ("done_sems", pltpu.SemaphoreType.DMA((count, occ_rows))),
            ]
        for s in passed:
            aliases["pass", s] = ("passed", s)
            ins.append((("pass", s), in_vmem(sends[s]), VMEM))
            outs.append((("passed", s), pltpu.VMEM(sends[s].shape, bf16), VMEM))
        if "token" in kept:
            ins.append(("before", in_vmem(kept["token"]), VMEM))
        outs.append(("token", pltpu.VMEM((8, 128), f32), VMEM))
        in_names, out_names = [name for name, _, _ in ins], [name for name, _, _ in outs]
        made = pl.pallas_call(
            functools.partial(
                step_kernel, in_names + out_names + [name for name, _ in scratch], tuple(makes), tuple(ends)
            ),
            in_specs=[spec for _, _, spec in ins],
            out_specs=[spec for _, _, spec in outs],
            out_shape=[shape for _, shape, _ in outs],
            scratch_shapes=[shape for _, shape in scratch],
            input_output_aliases={in_names.index(a): out_names.index(b) for a, b in aliases.items()},
            compiler_params=params,
        )(*[a for _, a, _ in ins])
        for name, a in zip(out_names, made, strict=True):
            if name[0] == "mixed":
                mixed[name[1:]] = a
            elif name[0] == "tile":
                sends[name[1:]] = a
            elif name[0] == "passed":
                sends[name[1]] = a
            else:
                kept[name] = a

    def start(which):
        for partner, k in which:
            arrived[partner, k] = swap(sends[partner, k], partner * vir + CORES * k) if partner or k else sends[0, 0]

    step(makes=[(0, 1)])
    start([(0, 3), (0, 2)])
    step(makes=[(1, 1), (0, 0), (1, 0), (2, 0)])
    start([(1, 3), (1, 2), (0, 0), (0, 1), (1, 0), (1, 1), (2, 0)])
    step(makes=[(2, 1), (3, 1), (3, 0)], ends=[(1, 0), (0, 1)], passed=[(2, 1)])
    start([(2, 3), (2, 2), (2, 1), (3, 0)])
    step(ends=[(0, 0), (1, 1)], passed=[(3, 2), (3, 1)])
    start([(3, 2), (3, 1)])
    step(ends=[(2, 1), (2, 0)], passed=[(3, 3)])
    start([(3, 3)])
    step(ends=[(3, 1), (3, 0)])
    return kept["result"]


def solution(mesh):
    occ, vir = mesh.shape["occ"], mesh.shape["vir"]

    def local(amplitudes, *others):
        occ_rows, _, rows, width = amplitudes.shape
        fits = (
            occ == 4
            and vir == 4 * CORES
            and rows % 16 == 0
            and width % 256 == 0
            and (occ_rows * occ_rows * CORES * rows) % 128 == 0
        )
        if fits:
            return paired(occ, vir, amplitudes, *others)
        return plain(amplitudes, *others)

    in_specs = (P("occ", None, "vir", None), P("vir", None), P(), P(), P(), P(), P())
    out_specs = P("occ", None, "vir", None)
    return jax.shard_map(local, mesh=mesh, in_specs=in_specs, out_specs=out_specs, check_vma=False)
```
